256 devices in a mesh: row: 64 (over y, z, core), grp: 4 (over x).
Axes of the slice: x: 4, y: 4, z: 8, core: 2. Of those that a mesh axis runs over, the one named last changes fastest.
Arguments:
- snapshots: float32 [256, 1048576], P('row', 'grp'), may hold values from -75 to 75, as said below
- lumped_mass: float32 [4, 262144], P('grp', 'row'), may hold values from 0.1 to 10
Outputs:
- pod_modes: float32 [256, 4, 262144], P(None, 'grp', 'row')
- triangle: float32 [256, 256], replicated
The draws below stay inside these ranges and needn't reach their ends.
Inputs may be any that keep to these rules, and one draw needn't show every extreme that they name: Real values; the snapshots have full rank.
All inputs are finite; a program needn't handle non-finite values.
Results may differ from the reference program's by a relative error of at most 0.0001.
Values sent between devices are 32-bit elements; how exact they have to be, the bound alone decides.
A program may use at most 128 MiB of HBM per device.

```python
import math
import jax
import jax.numpy as jnp
from jax import lax

K = 256
MG = 262144
M = 1048576
N_GRP = 4


def draw_snapshots(key, part):
    keys = jax.random.split(jax.random.fold_in(key, 11), 4)
    col_scale = jnp.exp(jax.random.uniform(keys[0], (K, 1), jnp.float32, 0.0, 2.302585))
    noise = jnp.clip(jax.random.normal(keys[1], (K, M), jnp.float32), -4.0, 4.0)
    common = 0.2
    field = jnp.clip(jax.random.normal(keys[2], (1, M), jnp.float32), -3.0, 3.0)
    loading = jnp.clip(jax.random.normal(keys[3], (K, 1), jnp.float32), -3.0, 3.0)
    return col_scale * (noise + common * loading * field)


def block_scale(own_key, shape, cuts, low, largest):
    def one(axis_at, blocks):
        steps = jax.random.uniform(jax.random.fold_in(jax.random.fold_in(own_key, 6), axis_at), (blocks,), jnp.float32, low / len(cuts), largest / len(cuts))
        return jnp.repeat(jnp.exp(steps), shape[axis_at] // blocks).reshape((-1,) + (1,) * (len(shape) - axis_at - 1))

    loudness = one(*cuts[0])
    for cut in cuts[1:]:
        loudness = loudness * one(*cut)
    return loudness


def setup_inputs(seed: int = 0) -> dict:
    streams_of = jax.random.split(jax.random.key(seed), 3)
    snapshots = draw_snapshots(jax.random.fold_in(streams_of[2], 71), 0)
    lumped_mass = jnp.clip(jnp.exp(math.log(10.0) - 4.6051702 * jax.random.uniform(streams_of[1], (N_GRP, MG), jnp.float32) ** block_scale(streams_of[1], (N_GRP, MG), ((0, 4), (1, 64)), -0.2, 0.2)), 0.1, 10.0)
    return dict(snapshots=snapshots, lumped_mass=lumped_mass)


def reference(snapshots, lumped_mass):
    width, count_all = snapshots.shape
    row_weight = jnp.sqrt(lumped_mass.reshape(1, count_all))
    block_rows = min(count_all, 65536)
    block_count = count_all // block_rows
    highest = lax.Precision.HIGHEST

    def add_block(index_step, gram_acc):
        start = (index_step * block_rows).astype(jnp.int32)
        columns = lax.dynamic_slice_in_dim(snapshots, start, block_rows, 1)
        columns = columns * lax.dynamic_slice_in_dim(row_weight, start, block_rows, 1)
        return gram_acc + lax.dot_general(columns, columns, (((1,), (1,)), ((), ())), precision=highest)
    gram = lax.fori_loop(0, block_count, add_block, jnp.zeros((width, width), jnp.float32)) / count_all
    factor_low = jnp.linalg.cholesky(gram)

    def solve_block(index_step, result):
        start = (index_step * block_rows).astype(jnp.int32)
        columns = lax.dynamic_slice_in_dim(snapshots, start, block_rows, 1)
        columns = columns * lax.dynamic_slice_in_dim(row_weight, start, block_rows, 1)
        solved = jax.scipy.linalg.solve_triangular(factor_low, columns, lower=True)
        return lax.dynamic_update_slice_in_dim(result, solved, start, 1)
    modes_flat = lax.fori_loop(0, block_count, solve_block, jnp.zeros((width, count_all), jnp.float32))
    groups = lumped_mass.shape[0]
    pod_modes = modes_flat.reshape(width, groups, count_all // groups)
    return (pod_modes, jnp.transpose(factor_low))
```

```python
import jax
import jax.numpy as jnp
from jax import lax
from jax.experimental import pallas as pl
from jax.experimental.pallas import tpu as pltpu
from jax.sharding import PartitionSpec as P

MESH = pl.DeviceIdType.MESH
F32 = jnp.float32
BF16 = jnp.bfloat16
K = 256
COORDS = 4096
TILES = 32
CHUNKS = 4
CT = TILES // CHUNKS
NT = (((1,), (1,)), ((), ()))
NN = (((1,), (0,)), ((), ()))


def split3(v):
    h = v.astype(BF16)
    r = v - h.astype(F32)
    m = r.astype(BF16)
    l = (r - m.astype(F32)).astype(BF16)
    return h, m, l


def gather_kernel(x_ref, w_ref, xs_ref, g_ref, buf, xs, gs, gx, half, parts, zp,
                  own_sem, in_send, in_recv, out_sem, red_send, red_recv):
    r = lax.axis_index("row")
    g = lax.axis_index("grp")
    y, z, c = r // 16, (r // 2) % 8, r % 2

    def dev(x_, y_, z_, c_):
        return (y_ * 16 + z_ * 2 + c_, x_)

    barrier = pltpu.get_barrier_semaphore()

    @pl.loop(1, 64)
    def _(o):
        pl.semaphore_signal(barrier, 1, device_id=(lax.rem(r + o, 64), g), device_id_type=MESH)

    for dx in range(1, 4):
        for dy in range(4):
            pl.semaphore_signal(barrier, 1, device_id=dev(lax.rem(g + dx, 4), lax.rem(y + dy, 4), z, c), device_id_type=MESH)
    pl.semaphore_wait(barrier, 63 + 12)

    rows = 128 // CHUNKS
    for ch in range(CHUNKS):
        @pl.loop(1, 64)
        def _(o):
            d = lax.rem(r + o, 64)
            pltpu.make_async_remote_copy(
                src_ref=x_ref.at[pl.ds(pl.multiple_of(d * 128 + ch * rows, rows), rows)],
                dst_ref=buf.at[r, pl.ds(ch * rows, rows)],
                send_sem=in_send, recv_sem=in_recv.at[ch],
                device_id=(d, g), device_id_type=MESH).start()
    own = pltpu.make_async_copy(x_ref.at[pl.ds(pl.multiple_of(r * 128, 128), 128)], buf.at[r], own_sem)
    own.start()
    own.wait()
    gs[...] = jnp.zeros_like(gs)
    gx[...] = jnp.zeros_like(gx)
    low = lax.broadcasted_iota(jnp.int32, (32, 8, 128), 1) < 4

    for ch in range(CHUNKS):
        arrived = buf.at[pl.ds(0, 63), pl.ds(0, rows)]
        pltpu.make_async_copy(arrived, arrived, in_recv.at[ch]).wait()

        @pl.loop(0, CT // 2)
        def _(q):
            pair = ch * (CT // 2) + q
            v = buf[:, pl.ds(pl.multiple_of(pair * 8, 8), 8), :].reshape(32, 2, 8, 128)
            even, odd = v[:, 0], v[:, 1]
            first = jnp.where(low, even, pltpu.roll(odd, 4, 1)).reshape(K, 128)
            second = jnp.where(low, pltpu.roll(even, 4, 1), odd).reshape(K, 128)
            sw = jnp.sqrt(w_ref[:, pl.ds(pl.multiple_of(pair * 256, 256), 256)])
            wide = jnp.concatenate([first, second], axis=1) * sw
            h, m, l = split3(wide)
            cols = pl.ds(pl.multiple_of(pair * 256, 256), 256)
            xs[0, :, cols] = h
            xs[1, :, cols] = m
            xs[2, :, cols] = l
            gs[...] += lax.dot_general(h, h, NT, preferred_element_type=F32) + lax.dot_general(m, m, NT, preferred_element_type=F32)
            gx[...] += lax.dot_general(h, m, NT, preferred_element_type=F32) + lax.dot_general(h, l, NT, preferred_element_type=F32)

        cols = pl.ds(ch * (COORDS // CHUNKS), COORDS // CHUNKS)
        pltpu.make_async_copy(xs.at[:, :, cols], xs_ref.at[:, :, cols], out_sem.at[ch]).start()

    cross = gx[...]
    gs[...] = (gs[...] + (cross + cross.T)) * (1.0 / (COORDS * 256))

    def send(src, dst, i, to):
        pltpu.make_async_remote_copy(src_ref=src, dst_ref=dst, send_sem=red_send.at[i], recv_sem=red_recv.at[i],
                                     device_id=to, device_id_type=MESH).start()

    def wait(ref, sem):
        pltpu.make_async_copy(ref, ref, sem).wait()

    partner = dev(g, y, z, 1 - c)
    send(gs.at[pl.ds(pl.multiple_of((1 - c) * 128, 128), 128)], half, 0, partner)
    wait(half, red_recv.at[0])
    half[...] += gs[pl.ds(pl.multiple_of(c * 128, 128), 128)]
    peers = [(dx, dy) for dx in range(4) for dy in range(4) if (dx, dy) != (0, 0)]
    peers.sort(key=lambda p: -(min(p[0], 4 - p[0]) + min(p[1], 4 - p[1])))
    for dx, dy in peers:
        px, py = lax.rem(g + dx, 4), lax.rem(y + dy, 4)
        send(half.at[pl.ds(pl.multiple_of((px * 4 + py) * 8, 8), 8)], parts.at[dx * 4 + dy - 1], 1, dev(px, py, z, c))
    wait(parts, red_recv.at[1])
    mine = half[pl.ds(pl.multiple_of((g * 4 + y) * 8, 8), 8)]
    for i in range(15):
        mine = mine + parts[i]
    zp[z] = mine
    for dz in (4, 3, 5, 2, 6, 1, 7):
        send(zp.at[z], zp.at[z], 2, dev(g, y, lax.rem(z + dz, 8), c))
    wait(zp.at[pl.ds(0, 7)], red_recv.at[2])
    total = zp[0]
    for i in range(1, 8):
        total = total + zp[i]
    here = pl.ds(pl.multiple_of(c * 128 + (g * 4 + y) * 8, 8), 8)
    g_ref[here] = total
    for dx, dy in peers:
        send(g_ref.at[here], g_ref.at[here], 3, dev(lax.rem(g + dx, 4), lax.rem(y + dy, 4), z, c))
    wait(g_ref.at[pl.ds(0, 120)], red_recv.at[3])
    there = pl.ds(pl.multiple_of(c * 128, 128), 128)
    send(g_ref.at[there], g_ref.at[there], 4, partner)
    wait(half, red_recv.at[4])

    wait(half, red_send.at[0])
    wait(parts, red_send.at[1])
    wait(zp.at[pl.ds(0, 7)], red_send.at[2])
    wait(g_ref.at[pl.ds(0, 120)], red_send.at[3])
    wait(half, red_send.at[4])
    wait(buf.at[pl.ds(0, 63)], in_send)
    for ch in range(CHUNKS):
        cols = pl.ds(ch * (COORDS // CHUNKS), COORDS // CHUNKS)
        pltpu.make_async_copy(xs.at[:, :, cols], xs_ref.at[:, :, cols], out_sem.at[ch]).wait()


B = 64
NB = K // B
STEP = 4


def eliminate(block):
    rows = lax.broadcasted_iota(jnp.int32, (B, 2 * B), 0)
    lanes = lax.broadcasted_iota(jnp.int32, (B, 2 * B), 1)
    m = jnp.concatenate([block, jnp.where(rows == lanes, 1.0, 0.0)[:, :B]], axis=1)
    tiles = [m[8 * t:8 * t + 8] for t in range(B // 8)]
    done = []
    full = (8, 2 * B)
    for j in range(0, B, STEP):
        t0, s0 = j // 8, j % 8
        top = tiles[t0]
        row = [jnp.broadcast_to(top[s0 + a:s0 + a + 1, :], full) for a in range(STEP)]
        d = {(a, b): jnp.broadcast_to(top[s0 + a:s0 + a + 1, j + b:j + b + 1], full) for a in range(STEP) for b in range(a + 1)}
        col = {(t, a): jnp.broadcast_to(tiles[t][:, j + a:j + a + 1], full) for t in range(t0, B // 8) for a in range(STEP)}
        inv = []
        for a in range(STEP):
            inv.append(1.0 / d[a, a])
            root = lax.rsqrt(d[a, a])
            root = root * (1.5 - 0.5 * d[a, a] * root * root)
            done.append((row[a] * root)[0:1])
            for b in range(a + 1, STEP):
                f = d[b, a] * inv[a]
                for k in range(b, STEP):
                    d[k, b] = d[k, b] - d[k, a] * f
                row[b] = row[b] - row[a] * f
                for t in range(t0, B // 8):
                    col[t, b] = col[t, b] - col[t, a] * f
        scaled = [row[a] * inv[a] for a in range(STEP)]
        for t in range(t0, B // 8):
            if 8 * t + 7 < j + STEP:
                continue
            for a in range(STEP):
                tiles[t] = tiles[t] - col[t, a] * scaled[a]
    return jnp.concatenate(done, axis=0)[:, B:]


def dot(a, b, dims):
    return lax.dot_general(a, b, dims, precision=lax.Precision.HIGHEST, preferred_element_type=F32)


def factor_kernel(g_ref, xs_ref, out_ref, tri_ref, a_ref, p_ref, xs, ob, in_sem, out_sem):
    pieces = 4
    wide = COORDS // pieces
    for i in range(pieces):
        cols = pl.ds(i * wide, wide)
        pltpu.make_async_copy(xs_ref.at[:, :, cols], xs.at[:, :, cols], in_sem.at[i]).start()
    a_ref[...] = g_ref[...]
    rows = lax.broadcasted_iota(jnp.int32, (K, K), 0)
    lanes = lax.broadcasted_iota(jnp.int32, (K, K), 1)
    p_ref[...] = jnp.where(rows == lanes, 1.0, 0.0)
    for j in range(NB):
        lo, hi = j * B, j * B + B
        inv = eliminate(a_ref[lo:hi, lo:hi])
        top_a = dot(inv, a_ref[lo:hi, :], NN)
        top_p = dot(inv, p_ref[lo:hi, :], NN)
        if j + 1 < NB:
            side = dot(a_ref[hi:, lo:hi], inv, NT)
            a_ref[hi:, :] -= dot(side, top_a, NN)
            p_ref[hi:, :] -= dot(side, top_p, NN)
        a_ref[lo:hi, :] = top_a
        p_ref[lo:hi, :] = top_p
    tri_ref[...] = jnp.where(lanes >= rows, a_ref[...], 0.0)
    wh, wm, wl = split3(p_ref[...])

    def mm(a, b):
        return lax.dot_general(a, b, NN, preferred_element_type=F32)

    for i in range(pieces):
        cols = pl.ds(i * wide, wide)
        pltpu.make_async_copy(xs_ref.at[:, :, cols], xs.at[:, :, cols], in_sem.at[i]).wait()

        @pl.loop(0, wide // 256)
        def _(q):
            n = i * (wide // 256) + q
            part = pl.ds(pl.multiple_of(n * 256, 256), 256)
            xh, xm, xl = xs[0, :, part], xs[1, :, part], xs[2, :, part]
            o = (mm(wh, xl) + mm(wl, xh) + mm(wm, xm)) + (mm(wh, xm) + mm(wm, xh)) + mm(wh, xh)
            ob[pl.ds(2 * n, K, stride=TILES), :] = o[:, :128]
            ob[pl.ds(2 * n + 1, K, stride=TILES), :] = o[:, 128:]

    copy = pltpu.make_async_copy(ob, out_ref, out_sem)
    copy.start()
    copy.wait()


def body(snapshots, lumped_mass):
    x = snapshots.reshape(4, 2048, 128).transpose(1, 0, 2).reshape(8192, 128)
    anywhere = pl.BlockSpec(memory_space=pl.ANY)
    hbm = pl.BlockSpec(memory_space=pltpu.HBM)
    vmem = pl.BlockSpec(memory_space=pltpu.VMEM)
    dma = pltpu.SemaphoreType.DMA
    xs, gram = pl.pallas_call(
        gather_kernel,
        name="gather_gram",
        out_shape=(jax.ShapeDtypeStruct((3, K, COORDS), BF16), jax.ShapeDtypeStruct((K, K), F32)),
        in_specs=[hbm, vmem],
        out_specs=(anywhere, vmem),
        scratch_shapes=[
            pltpu.VMEM((64, 128, 128), F32),
            pltpu.VMEM((3, K, COORDS), BF16),
            pltpu.VMEM((K, K), F32),
            pltpu.VMEM((K, K), F32),
            pltpu.VMEM((128, K), F32),
            pltpu.VMEM((15, 8, K), F32),
            pltpu.VMEM((8, 8, K), F32),
            dma, dma, dma((CHUNKS,)), dma((CHUNKS,)), dma((5,)), dma((5,)),
        ],
        compiler_params=pltpu.CompilerParams(collective_id=0, has_side_effects=True, vmem_limit_bytes=58 * 2**20),
    )(x, lumped_mass)
    out, tri = pl.pallas_call(
        factor_kernel,
        name="factor_project",
        out_shape=(jax.ShapeDtypeStruct((8192, 128), F32), jax.ShapeDtypeStruct((K, K), F32)),
        in_specs=[vmem, anywhere],
        out_specs=(anywhere, vmem),
        scratch_shapes=[
            pltpu.VMEM((K, K), F32),
            pltpu.VMEM((K, K), F32),
            pltpu.VMEM((3, K, COORDS), BF16),
            pltpu.VMEM((8192, 128), F32),
            dma((4,)), dma,
        ],
        compiler_params=pltpu.CompilerParams(vmem_limit_bytes=58 * 2**20),
    )(gram, xs)
    return out.reshape(K, 1, COORDS), tri


def solution(mesh):
    return jax.shard_map(
        body,
        mesh=mesh,
        in_specs=(P("row", "grp"), P("grp", "row")),
        out_specs=(P(None, "grp", "row"), P()),
        check_vma=False,
    )
```

```python
import jax
import jax.numpy as jnp
from jax import lax
from jax.experimental import pallas as pl
from jax.experimental.pallas import tpu as pltpu
from jax.sharding import PartitionSpec as P

MESH = pl.DeviceIdType.MESH
F32 = jnp.float32
BF16 = jnp.bfloat16
K = 256
COORDS = 4096
TILES = 32
FILL = 3
HELD = 8
LAG = 5
B = 64
STEP = 8
SCALE = 1.0 / 1048576
NT = (((1,), (1,)), ((), ()))
NN = (((1,), (0,)), ((), ()))


def split3(v):
    h = v.astype(BF16)
    r = v - h.astype(F32)
    m = r.astype(BF16)
    l = (r - m.astype(F32)).astype(BF16)
    return h, m, l


def mm(a, b, dims):
    return lax.dot_general(a, b, dims, preferred_element_type=F32)


def dot(a, b, dims):
    return lax.dot_general(a, b, dims, precision=lax.Precision.HIGHEST, preferred_element_type=F32)


def eliminate(block):
    rows = lax.broadcasted_iota(jnp.int32, (B, B), 0)
    lanes = lax.broadcasted_iota(jnp.int32, (B, B), 1)
    m = jnp.concatenate([block, jnp.where(rows == lanes, 1.0, 0.0)], axis=1)
    tiles = [m[8 * t:8 * t + 8] for t in range(B // 8)]
    done = []
    full = (8, 2 * B)
    for j in range(0, B, STEP):
        t0, s0 = j // 8, j % 8
        top = tiles[t0]
        row = [jnp.broadcast_to(top[s0 + a:s0 + a + 1, :], full) for a in range(STEP)]
        d = {(a, b): jnp.broadcast_to(top[s0 + a:s0 + a + 1, j + b:j + b + 1], full) for a in range(STEP) for b in range(a + 1)}
        live = [t for t in range(t0, B // 8) if 8 * t + 7 >= j + STEP]
        col = {(t, a): jnp.broadcast_to(tiles[t][:, j + a:j + a + 1], full) for t in live for a in range(STEP)}
        inv = []
        for a in range(STEP):
            inv.append(1.0 / d[a, a])
            root = lax.rsqrt(d[a, a])
            root = root * (1.5 - 0.5 * d[a, a] * root * root)
            done.append((row[a] * root)[0:1])
            for b in range(a + 1, STEP):
                f = d[b, a] * inv[a]
                for k in range(b, STEP):
                    d[k, b] = d[k, b] - d[k, a] * f
                row[b] = row[b] - row[a] * f
                for t in live:
                    col[t, b] = col[t, b] - col[t, a] * f
        scaled = [row[a] * inv[a] for a in range(STEP)]
        for t in live:
            for a in range(STEP):
                tiles[t] = tiles[t] - col[t, a] * scaled[a]
    return jnp.concatenate(done, axis=0)


def keep_upper(t):
    rows = lax.broadcasted_iota(jnp.int32, t.shape, 0)
    lanes = lax.broadcasted_iota(jnp.int32, t.shape, 1)
    return jnp.where(lanes >= rows, t, 0.0)


def pod_kernel(x_ref, w_ref, out_ref, tri_ref, buf, stage, xs, gram, p_ref, tmp, pack, parts, zparts, res,
               y_send, y_recv, z_send, z_recv, red_send, red_recv):
    r = lax.axis_index("row")
    g = lax.axis_index("grp")
    y, zc = r // 16, lax.rem(r, 16)
    phase_of = jnp.where(y < 2, 0, y - 1)

    def dev(x_, y_, zc_):
        return (y_ * 16 + zc_, x_)

    plane = [(dx, dy) for dx in range(4) for dy in range(4) if (dx, dy) != (0, 0)]
    plane.sort(key=lambda p: -(min(p[0], 4 - p[0]) + min(p[1], 4 - p[1])))

    barrier = pltpu.get_barrier_semaphore()

    @pl.loop(1, 16)
    def _(o):
        pl.semaphore_signal(barrier, 1, device_id=dev(g, y, lax.rem(zc + o, 16)), device_id_type=MESH)

    for dx, dy in plane:
        pl.semaphore_signal(barrier, 1, device_id=dev(lax.rem(g + dx, 4), lax.rem(y + dy, 4), zc), device_id_type=MESH)
    pl.semaphore_wait(barrier, 30)

    def block(plane_y, b):
        return x_ref.at[pl.ds(pl.multiple_of((plane_y * 16 + b) * 128, 128), 128)]

    def target(i):
        return lax.rem(zc + lax.rem(i * 7, 15) + 1, 16)

    def along_y(i):
        for d in (1, 3, 2):
            to = lax.rem(y + d, 4)
            pltpu.make_async_remote_copy(
                src_ref=block(to, target(i)), dst_ref=stage.at[d - 1, i], send_sem=y_send, recv_sem=y_recv.at[d - 1, i],
                device_id=dev(g, to, zc), device_id_type=MESH).start()

    def along_z(src, slot, i, which):
        pltpu.make_async_remote_copy(
            src_ref=src, dst_ref=buf.at[slot], send_sem=z_send, recv_sem=z_recv.at[which],
            device_id=dev(g, y, target(i)), device_id_type=MESH).start()

    def forward(d, i, which):
        pltpu.make_async_copy(stage.at[0, 0], stage.at[d - 1, i], y_recv.at[d - 1, i]).wait()
        along_z(stage.at[d - 1, i], lax.rem(y - d + 4, 4) * 16 + zc, i, which)

    def own(i, which):
        along_z(block(y, target(i)), r, i, which)

    def own_column():
        for d in (1, 3, 2):
            to = lax.rem(y + d, 4)
            pltpu.make_async_remote_copy(
                src_ref=block(to, zc), dst_ref=buf.at[r], send_sem=y_send, recv_sem=z_recv.at[phase_of],
                device_id=dev(g, to, zc), device_id_type=MESH).start()
        pltpu.make_async_copy(block(y, zc), buf.at[r], z_recv.at[phase_of]).start()

    @pl.when(y < 2)
    def _():
        other = jnp.where(y == 0, 3, 1)

        @pl.loop(0, LAG)
        def _(i):
            along_y(i)
            own(i, 0)

        @pl.loop(LAG, 15)
        def _(i):
            along_y(i)
            own(i, 0)
            forward(other, i - LAG, 0)

        own_column()

        @pl.loop(15 - LAG, 15)
        def _(i):
            forward(other, i, 0)

    @pl.when(y >= 2)
    def _():
        @pl.loop(0, FILL)
        def _(i):
            along_y(i)
            own(i, phase_of)

        @pl.loop(0, 15)
        def _(i):
            forward(y, i, 0)
            forward(y - 1, i, 0)

            @pl.when(i + FILL < 15)
            def _():
                along_y(i + FILL)

        own_column()

    def send_plane(src, lo, hi):
        d = lax.rem(y - src + 4, 4)

        @pl.when(d != 0)
        def _():
            @pl.loop(lo, hi)
            def _(i):
                forward(d, i, src - 1)

        if hi > FILL:
            @pl.when(d == 0)
            def _():
                @pl.loop(lo, hi)
                def _(i):
                    own(i, src - 1)

    def wait(ref, sem):
        pltpu.make_async_copy(ref, ref, sem).wait()

    def weighted(lo, n, pair):
        v = buf[lo // 4:(lo + n) // 4, pl.ds(pl.multiple_of(pair * 8, 8), 8), :].reshape(n // 8, 2, 8, 128)
        even, odd = v[:, 0], v[:, 1]
        low = lax.broadcasted_iota(jnp.int32, even.shape, 1) < 4
        left = jnp.where(low, even, pltpu.roll(odd, 4, 1)).reshape(n, 128)
        right = jnp.where(low, pltpu.roll(even, 4, 1), odd).reshape(n, 128)
        cols = pl.ds(pl.multiple_of(pair * 256, 256), 256)
        for k, v in enumerate(split3(jnp.concatenate([left, right], axis=1) * jnp.sqrt(w_ref[:, cols]))):
            xs[k, lo:lo + n, cols] = v

    def rows_gram(lo, n):
        end = lo + n
        gram[:3 * n, :end] = jnp.zeros((3 * n, end), F32)

        @pl.loop(0, 4)
        def _(quad):
            for p in range(4):
                weighted(lo, n, quad * 4 + p)
            cols = pl.ds(pl.multiple_of(quad * 1024, 1024), 1024)
            h, m, l = xs[0, lo:end, cols], xs[1, lo:end, cols], xs[2, lo:end, cols]
            gram[:3 * n, :end] += mm(jnp.concatenate([h, m, l], axis=0), xs[0, :end, cols], NT)
            gram[:2 * n, :end] += mm(jnp.concatenate([h, m], axis=0), xs[1, :end, cols], NT)
            gram[:n, :end] += mm(h, xs[2, :end, cols], NT)

        return (gram[2 * n:3 * n, :end] + gram[n:2 * n, :end]) + gram[:n, :end]

    def send(src, dst, i, to):
        pltpu.make_async_remote_copy(src_ref=src, dst_ref=dst, send_sem=red_send.at[i], recv_sem=red_recv.at[i],
                                     device_id=to, device_id_type=MESH).start()

    def part(ref, k, px, py):
        return ref.at[k, pl.ds(pl.multiple_of((px * 4 + py) * 8, 8), 8)]

    def sum_start(k):
        for dx, dy in plane:
            px, py = lax.rem(g + dx, 4), lax.rem(y + dy, 4)
            send(part(pack, k, px, py), parts.at[k, dx * 4 + dy - 1], 3 * k, dev(px, py, zc))

    def sum_second(k):
        wait(parts.at[k], red_recv.at[3 * k])
        mine = part(pack, k, g, y)[...]
        for i in range(15):
            mine = mine + parts[k, i]
        zparts[k, zc] = mine

        @pl.loop(0, 15)
        def _(i):
            send(zparts.at[k, zc], zparts.at[k, zc], 3 * k + 1, dev(g, y, target(i)))

    def sum_third(k):
        wait(zparts.at[k, pl.ds(0, 15)], red_recv.at[3 * k + 1])
        total = zparts[k, 0]
        for i in range(1, 16):
            total = total + zparts[k, i]
        here = part(res, k, g, y)
        here[...] = total * SCALE
        for dx, dy in plane:
            send(here, here, 3 * k + 2, dev(lax.rem(g + dx, 4), lax.rem(y + dy, 4), zc))

    def sum_done(k):
        wait(parts.at[k], red_recv.at[3 * k + 2])

    def reduce_end(k):
        wait(parts.at[k], red_send.at[3 * k])
        wait(parts.at[k], red_send.at[3 * k + 1])
        wait(parts.at[k], red_send.at[3 * k + 2])

    def factor_rows(lo, strip, corner):
        hi = lo + B
        above = p_ref[:lo, :lo]
        side = dot(strip, above, NT)
        both = eliminate(corner - dot(side, side, NT))
        inv = both[:, B:]
        tri_ref[lo:hi, lo:hi] = keep_upper(both[:, :B])
        tri_ref[:lo, lo:hi] = dot(above, strip, NT)
        p_ref[lo:hi, :lo] = -dot(inv, dot(side, above, NN), NN)
        p_ref[lo:hi, lo:hi] = inv

    def project(w3, lo, n, q):
        end = lo + n
        wh, wm, wl = w3
        w_hml = jnp.concatenate([wh, wm, wl], axis=0)
        w_hm = jnp.concatenate([wh, wm], axis=0)
        for i in range(4):
            cols = pl.ds(q * 1024 + i * 256, 256)
            s = mm(w_hml, xs[0, :end, cols], NN)
            t = mm(w_hm, xs[1, :end, cols], NN)
            u = mm(wh, xs[2, :end, cols], NN)
            tmp[:n, i * 256:i * 256 + 256] = (s[2 * n:] + t[n:] + u) + (s[n:2 * n] + t[:n]) + s[:n]
        v = [tmp[:n, k * 128:k * 128 + 128].reshape(n // 8, 8, 128) for k in range(8)]
        sub = lax.broadcasted_iota(jnp.int32, (n // 8, 8, 128), 1)
        for step in (4, 2, 1):
            keep = (sub & step) == 0
            for k in range(8):
                if k & step == 0:
                    a, b = v[k], v[k + step]
                    v[k] = jnp.where(keep, a, pltpu.roll(b, step, 1))
                    v[k + step] = jnp.where(keep, pltpu.roll(a, 8 - step, 1), b)
        for s in range(8):
            out_ref[lo // 8:end // 8, s, 8 * q:8 * q + 8, :] = v[s]

    p_ref[...] = jnp.zeros_like(p_ref)
    tri_ref[...] = jnp.zeros_like(tri_ref)
    send_plane(2, 0, FILL)
    send_plane(2, FILL, 15)

    wait(buf.at[pl.ds(0, 32)], z_recv.at[0])
    pack[0] = rows_gram(0, 128)
    sum_start(0)
    send_plane(3, 0, FILL)
    send_plane(3, FILL, HELD)

    wait(buf.at[pl.ds(32, 16)], z_recv.at[1])
    strip = rows_gram(128, B)
    pack[1, :B] = strip[:, :128]
    pack[1, B:, :B] = strip[:, 128:]
    pack[1, B:, B:] = jnp.zeros((B, B), F32)
    sum_second(0)
    sum_start(1)
    send_plane(3, HELD, 15)
    sum_third(0)
    sum_second(1)

    wait(buf.at[pl.ds(48, 16)], z_recv.at[2])
    strip = rows_gram(192, B)
    pack[2, :B] = strip[:, :128]
    pack[2, B:] = strip[:, 128:]
    sum_start(2)
    sum_third(1)
    sum_done(0)
    both = eliminate(res[0, :B, :B])
    p_ref[:B, :B] = both[:, B:]
    tri_ref[:B, :B] = keep_upper(both[:, :B])
    sum_second(2)
    factor_rows(B, res[0, B:, :B], res[0, B:, B:])
    sum_third(2)
    sum_done(1)
    factor_rows(128, res[1, :B], res[1, B:, :B])
    w3 = split3(p_ref[:192, :192])
    for q in range(4):
        project(w3, 0, 192, q)
    sum_done(2)
    factor_rows(192, jnp.concatenate([res[2, :B], res[2, B:, :B]], axis=1), res[2, B:, B:])
    w3 = split3(p_ref[192:, :])
    for q in range(4):
        project(w3, 192, B, q)

    for k in range(3):
        reduce_end(k)
    wait(buf.at[pl.ds(0, 48)], y_send)
    wait(buf.at[pl.ds(0, 60)], z_send)


def store_kernel(modes_ref, upper_ref, out_ref, tri_ref, sems):
    one = pltpu.make_async_copy(modes_ref, out_ref, sems.at[0])
    two = pltpu.make_async_copy(upper_ref, tri_ref, sems.at[1])
    one.start()
    two.start()
    one.wait()
    two.wait()


def body(snapshots, lumped_mass):
    x = snapshots.reshape(4, 2048, 128).transpose(1, 0, 2).reshape(8192, 128)
    anywhere = pl.BlockSpec(memory_space=pl.ANY)
    vmem = pl.BlockSpec(memory_space=pltpu.VMEM)
    dma = pltpu.SemaphoreType.DMA

    def room(*shape):
        return pltpu.VMEM(shape, F32)

    modes, upper = pl.pallas_call(
        pod_kernel,
        name="pod",
        out_shape=(jax.ShapeDtypeStruct((32, 8, TILES, 128), F32), jax.ShapeDtypeStruct((K, K), F32)),
        in_specs=[anywhere, vmem],
        out_specs=(vmem, vmem),
        scratch_shapes=[
            room(64, 128, 128), room(3, 15, 128, 128), pltpu.VMEM((3, K, COORDS), BF16),
            room(384, K), room(K, K), room(192, 1024),
            room(3, 128, 128), room(3, 15, 8, 128), room(3, 16, 8, 128), room(3, 128, 128),
            dma, dma((3, 15)), dma, dma((3,)), dma((9,)), dma((9,)),
        ],
        compiler_params=pltpu.CompilerParams(collective_id=0, has_side_effects=True, vmem_limit_bytes=VMEM_LIMIT),
    )(x, lumped_mass)
    out, tri = pl.pallas_call(
        store_kernel,
        name="store",
        out_shape=(jax.ShapeDtypeStruct(modes.shape, F32), jax.ShapeDtypeStruct((K, K), F32)),
        in_specs=[anywhere, anywhere],
        out_specs=(anywhere, anywhere),
        scratch_shapes=[dma((2,))],
        compiler_params=pltpu.CompilerParams(vmem_limit_bytes=STORE_LIMIT),
    )(modes, upper)
    return out.reshape(K, 1, COORDS), tri


STORE_LIMIT = 40 * 2**20
VMEM_LIMIT = 47 * 2**20


def solution(mesh):
    return jax.shard_map(
        body,
        mesh=mesh,
        in_specs=(P("row", "grp"), P("grp", "row")),
        out_specs=(P(None, "grp", "row"), P()),
        check_vma=False,
    )
```

```python
import jax
import jax.numpy as jnp
from jax import lax
from jax.experimental import pallas as pl
from jax.experimental.pallas import tpu as pltpu
from jax.sharding import PartitionSpec as P

MESH = pl.DeviceIdType.MESH
F32 = jnp.float32
BF16 = jnp.bfloat16
K = 256
COORDS = 4096
TILES = 32
FILL = 6
HELD = 9
LAG = 5
B = 64
STEP = 8
SCALE = 1.0 / 1048576
NT = (((1,), (1,)), ((), ()))
NN = (((1,), (0,)), ((), ()))


def split3(v):
    h = v.astype(BF16)
    r = v - h.astype(F32)
    m = r.astype(BF16)
    l = (r - m.astype(F32)).astype(BF16)
    return h, m, l


def mm(a, b, dims):
    return lax.dot_general(a, b, dims, preferred_element_type=F32)


def dot(a, b, dims):
    return lax.dot_general(a, b, dims, precision=lax.Precision.HIGHEST, preferred_element_type=F32)


def eliminate(block):
    rows = lax.broadcasted_iota(jnp.int32, (B, B), 0)
    lanes = lax.broadcasted_iota(jnp.int32, (B, B), 1)
    m = jnp.concatenate([block, jnp.where(rows == lanes, 1.0, 0.0)], axis=1)
    tiles = [m[8 * t:8 * t + 8] for t in range(B // 8)]
    done = []
    full = (8, 2 * B)
    for j in range(0, B, STEP):
        t0, s0 = j // 8, j % 8
        top = tiles[t0]
        row = [jnp.broadcast_to(top[s0 + a:s0 + a + 1, :], full) for a in range(STEP)]
        d = {(a, b): jnp.broadcast_to(top[s0 + a:s0 + a + 1, j + b:j + b + 1], full) for a in range(STEP) for b in range(a + 1)}
        live = [t for t in range(t0, B // 8) if 8 * t + 7 >= j + STEP]
        col = {(t, a): jnp.broadcast_to(tiles[t][:, j + a:j + a + 1], full) for t in live for a in range(STEP)}
        inv = []
        for a in range(STEP):
            inv.append(1.0 / d[a, a])
            root = lax.rsqrt(d[a, a])
            root = root * (1.5 - 0.5 * d[a, a] * root * root)
            done.append((row[a] * root)[0:1])
            for b in range(a + 1, STEP):
                f = d[b, a] * inv[a]
                for k in range(b, STEP):
                    d[k, b] = d[k, b] - d[k, a] * f
                row[b] = row[b] - row[a] * f
                for t in live:
                    col[t, b] = col[t, b] - col[t, a] * f
        scaled = [row[a] * inv[a] for a in range(STEP)]
        for t in live:
            for a in range(STEP):
                tiles[t] = tiles[t] - col[t, a] * scaled[a]
    return jnp.concatenate(done, axis=0)


def keep_upper(t):
    rows = lax.broadcasted_iota(jnp.int32, t.shape, 0)
    lanes = lax.broadcasted_iota(jnp.int32, t.shape, 1)
    return jnp.where(lanes >= rows, t, 0.0)


def pod_kernel(x_ref, w_ref, out_ref, tri_ref, buf, stage, xs, gram, p_ref, tmp, pack, parts, zparts, res,
               y_send, y_recv, z_send, z_recv, red_send, red_recv):
    r = lax.axis_index("row")
    g = lax.axis_index("grp")
    y, zc = r // 16, lax.rem(r, 16)
    phase_of = jnp.where(y < 2, 0, y - 1)

    def dev(x_, y_, zc_):
        return (y_ * 16 + zc_, x_)

    plane = [(dx, dy) for dx in range(4) for dy in range(4) if (dx, dy) != (0, 0)]
    plane.sort(key=lambda p: -(min(p[0], 4 - p[0]) + min(p[1], 4 - p[1])))

    barrier = pltpu.get_barrier_semaphore()

    @pl.loop(1, 16)
    def _(o):
        pl.semaphore_signal(barrier, 1, device_id=dev(g, y, lax.rem(zc + o, 16)), device_id_type=MESH)

    for dx, dy in plane:
        pl.semaphore_signal(barrier, 1, device_id=dev(lax.rem(g + dx, 4), lax.rem(y + dy, 4), zc), device_id_type=MESH)
    pl.semaphore_wait(barrier, 30)

    def block(plane_y, b):
        return x_ref.at[pl.ds(pl.multiple_of((plane_y * 16 + b) * 128, 128), 128)]

    def target(i):
        return lax.rem(zc + lax.rem(i * 7, 15) + 1, 16)

    def along_y(i):
        for d in (1, 3, 2):
            to = lax.rem(y + d, 4)
            pltpu.make_async_remote_copy(
                src_ref=block(to, target(i)), dst_ref=stage.at[d - 1, i], send_sem=y_send, recv_sem=y_recv.at[d - 1, i],
                device_id=dev(g, to, zc), device_id_type=MESH).start()

    def along_z(src, slot, i, which):
        pltpu.make_async_remote_copy(
            src_ref=src, dst_ref=buf.at[slot], send_sem=z_send, recv_sem=z_recv.at[which],
            device_id=dev(g, y, target(i)), device_id_type=MESH).start()

    def forward(d, i, which):
        pltpu.make_async_copy(stage.at[0, 0], stage.at[d - 1, i], y_recv.at[d - 1, i]).wait()
        along_z(stage.at[d - 1, i], lax.rem(y - d + 4, 4) * 16 + zc, i, which)

    def own(i, which):
        along_z(block(y, target(i)), r, i, which)

    def own_column():
        for d in (1, 3, 2):
            to = lax.rem(y + d, 4)
            pltpu.make_async_remote_copy(
                src_ref=block(to, zc), dst_ref=buf.at[r], send_sem=y_send, recv_sem=z_recv.at[phase_of],
                device_id=dev(g, to, zc), device_id_type=MESH).start()
        pltpu.make_async_copy(block(y, zc), buf.at[r], z_recv.at[phase_of]).start()

    @pl.when(y < 2)
    def _():
        other = jnp.where(y == 0, 3, 1)

        @pl.loop(0, LAG)
        def _(i):
            along_y(i)
            own(i, 0)

        @pl.loop(LAG, 15)
        def _(i):
            along_y(i)
            own(i, 0)
            forward(other, i - LAG, 0)

        own_column()

        @pl.loop(15 - LAG, 15)
        def _(i):
            forward(other, i, 0)

    @pl.when(y >= 2)
    def _():
        @pl.loop(0, FILL)
        def _(i):
            along_y(i)
            own(i, phase_of)

        @pl.loop(0, 15)
        def _(i):
            forward(y, i, 0)
            forward(y - 1, i, 0)

            @pl.when(i + FILL < 15)
            def _():
                along_y(i + FILL)

        own_column()

    def send_plane(src, lo, hi):
        d = lax.rem(y - src + 4, 4)

        @pl.when(d != 0)
        def _():
            @pl.loop(lo, hi)
            def _(i):
                forward(d, i, src - 1)

        if hi > FILL:
            @pl.when(d == 0)
            def _():
                @pl.loop(lo, hi)
                def _(i):
                    own(i, src - 1)

    def wait(ref, sem):
        pltpu.make_async_copy(ref, ref, sem).wait()

    def weighted(lo, n, pair):
        v = buf[lo // 4:(lo + n) // 4, pl.ds(pl.multiple_of(pair * 8, 8), 8), :].reshape(n // 8, 2, 8, 128)
        even, odd = v[:, 0], v[:, 1]
        low = lax.broadcasted_iota(jnp.int32, even.shape, 1) < 4
        left = jnp.where(low, even, pltpu.roll(odd, 4, 1)).reshape(n, 128)
        right = jnp.where(low, pltpu.roll(even, 4, 1), odd).reshape(n, 128)
        cols = pl.ds(pl.multiple_of(pair * 256, 256), 256)
        for k, v in enumerate(split3(jnp.concatenate([left, right], axis=1) * jnp.sqrt(w_ref[:, cols]))):
            xs[k, lo:lo + n, cols] = v

    def rows_gram(lo, n):
        end = lo + n
        gram[:3 * n, :end] = jnp.zeros((3 * n, end), F32)

        @pl.loop(0, 4)
        def _(quad):
            for p in range(4):
                weighted(lo, n, quad * 4 + p)
            cols = pl.ds(pl.multiple_of(quad * 1024, 1024), 1024)
            h, m, l = xs[0, lo:end, cols], xs[1, lo:end, cols], xs[2, lo:end, cols]
            gram[:3 * n, :end] += mm(jnp.concatenate([h, m, l], axis=0), xs[0, :end, cols], NT)
            gram[:2 * n, :end] += mm(jnp.concatenate([h, m], axis=0), xs[1, :end, cols], NT)
            gram[:n, :end] += mm(h, xs[2, :end, cols], NT)

        return (gram[2 * n:3 * n, :end] + gram[n:2 * n, :end]) + gram[:n, :end]

    def send(src, dst, i, to):
        pltpu.make_async_remote_copy(src_ref=src, dst_ref=dst, send_sem=red_send.at[i], recv_sem=red_recv.at[i],
                                     device_id=to, device_id_type=MESH).start()

    def part(ref, k, px, py):
        return ref.at[k, pl.ds(pl.multiple_of((px * 4 + py) * 8, 8), 8)]

    def sum_start(k):
        for dx, dy in plane:
            px, py = lax.rem(g + dx, 4), lax.rem(y + dy, 4)
            send(part(pack, k, px, py), parts.at[k, dx * 4 + dy - 1], 3 * k, dev(px, py, zc))

    def sum_second(k):
        wait(parts.at[k], red_recv.at[3 * k])
        mine = part(pack, k, g, y)[...]
        for i in range(15):
            mine = mine + parts[k, i]
        zparts[k, zc] = mine

        @pl.loop(0, 15)
        def _(i):
            send(zparts.at[k, zc], zparts.at[k, zc], 3 * k + 1, dev(g, y, target(i)))

    def sum_third(k):
        wait(zparts.at[k, pl.ds(0, 15)], red_recv.at[3 * k + 1])
        total = zparts[k, 0]
        for i in range(1, 16):
            total = total + zparts[k, i]
        here = part(res, k, g, y)
        here[...] = total * SCALE
        for dx, dy in plane:
            send(here, here, 3 * k + 2, dev(lax.rem(g + dx, 4), lax.rem(y + dy, 4), zc))

    def sum_done(k):
        wait(parts.at[k], red_recv.at[3 * k + 2])

    def reduce_end(k):
        wait(parts.at[k], red_send.at[3 * k])
        wait(parts.at[k], red_send.at[3 * k + 1])
        wait(parts.at[k], red_send.at[3 * k + 2])

    def factor_rows(lo, strip, corner):
        hi = lo + B
        above = p_ref[:lo, :lo]
        side = dot(strip, above, NT)
        both = eliminate(corner - dot(side, side, NT))
        inv = both[:, B:]
        tri_ref[lo:hi, lo:hi] = keep_upper(both[:, :B])
        tri_ref[:lo, lo:hi] = dot(above, strip, NT)
        p_ref[lo:hi, :lo] = -dot(inv, dot(side, above, NN), NN)
        p_ref[lo:hi, lo:hi] = inv

    def project(w3, lo, n, q):
        end = lo + n
        wh, wm, wl = w3
        w_hml = jnp.concatenate([wh, wm, wl], axis=0)
        w_hm = jnp.concatenate([wh, wm], axis=0)
        for i in range(4):
            cols = pl.ds(q * 1024 + i * 256, 256)
            s = mm(w_hml, xs[0, :end, cols], NN)
            t = mm(w_hm, xs[1, :end, cols], NN)
            u = mm(wh, xs[2, :end, cols], NN)
            tmp[:n, i * 256:i * 256 + 256] = (s[2 * n:] + t[n:] + u) + (s[n:2 * n] + t[:n]) + s[:n]
        v = [tmp[:n, k * 128:k * 128 + 128].reshape(n // 8, 8, 128) for k in range(8)]
        sub = lax.broadcasted_iota(jnp.int32, (n // 8, 8, 128), 1)
        for step in (4, 2, 1):
            keep = (sub & step) == 0
            for k in range(8):
                if k & step == 0:
                    a, b = v[k], v[k + step]
                    v[k] = jnp.where(keep, a, pltpu.roll(b, step, 1))
                    v[k + step] = jnp.where(keep, pltpu.roll(a, 8 - step, 1), b)
        for s in range(8):
            out_ref[lo // 8:end // 8, s, 8 * q:8 * q + 8, :] = v[s]

    p_ref[...] = jnp.zeros_like(p_ref)
    tri_ref[...] = jnp.zeros_like(tri_ref)
    send_plane(2, 0, FILL)
    send_plane(2, FILL, 15)

    wait(buf.at[pl.ds(0, 32)], z_recv.at[0])
    pack[0] = rows_gram(0, 128)
    sum_start(0)
    send_plane(3, 0, FILL)
    send_plane(3, FILL, HELD)

    wait(buf.at[pl.ds(32, 16)], z_recv.at[1])
    strip = rows_gram(128, B)
    pack[1, :B] = strip[:, :128]
    pack[1, B:, :B] = strip[:, 128:]
    pack[1, B:, B:] = jnp.zeros((B, B), F32)
    sum_second(0)
    sum_start(1)
    send_plane(3, HELD, 15)
    sum_third(0)
    sum_second(1)

    wait(buf.at[pl.ds(48, 16)], z_recv.at[2])
    strip = rows_gram(192, B)
    pack[2, :B] = strip[:, :128]
    pack[2, B:] = strip[:, 128:]
    sum_start(2)
    sum_third(1)
    sum_done(0)
    both = eliminate(res[0, :B, :B])
    p_ref[:B, :B] = both[:, B:]
    tri_ref[:B, :B] = keep_upper(both[:, :B])
    factor_rows(B, res[0, B:, :B], res[0, B:, B:])
    sum_second(2)
    sum_done(1)
    factor_rows(128, res[1, :B], res[1, B:, :B])
    sum_third(2)
    w3 = split3(p_ref[:192, :192])
    for q in range(4):
        project(w3, 0, 192, q)
    sum_done(2)
    factor_rows(192, jnp.concatenate([res[2, :B], res[2, B:, :B]], axis=1), res[2, B:, B:])
    w3 = split3(p_ref[192:, :])
    for q in range(4):
        project(w3, 192, B, q)

    for k in range(3):
        reduce_end(k)
    wait(buf.at[pl.ds(0, 48)], y_send)
    wait(buf.at[pl.ds(0, 60)], z_send)


def store_kernel(modes_ref, upper_ref, out_ref, tri_ref, sems):
    one = pltpu.make_async_copy(modes_ref, out_ref, sems.at[0])
    two = pltpu.make_async_copy(upper_ref, tri_ref, sems.at[1])
    one.start()
    two.start()
    one.wait()
    two.wait()


def body(snapshots, lumped_mass):
    x = snapshots.reshape(4, 2048, 128).transpose(1, 0, 2).reshape(8192, 128)
    anywhere = pl.BlockSpec(memory_space=pl.ANY)
    vmem = pl.BlockSpec(memory_space=pltpu.VMEM)
    dma = pltpu.SemaphoreType.DMA

    def room(*shape):
        return pltpu.VMEM(shape, F32)

    modes, upper = pl.pallas_call(
        pod_kernel,
        name="pod",
        out_shape=(jax.ShapeDtypeStruct((32, 8, TILES, 128), F32), jax.ShapeDtypeStruct((K, K), F32)),
        in_specs=[anywhere, vmem],
        out_specs=(vmem, vmem),
        scratch_shapes=[
            room(64, 128, 128), room(3, 15, 128, 128), pltpu.VMEM((3, K, COORDS), BF16),
            room(384, K), room(K, K), room(192, 1024),
            room(3, 128, 128), room(3, 15, 8, 128), room(3, 16, 8, 128), room(3, 128, 128),
            dma, dma((3, 15)), dma, dma((3,)), dma((9,)), dma((9,)),
        ],
        compiler_params=pltpu.CompilerParams(collective_id=0, has_side_effects=True, vmem_limit_bytes=VMEM_LIMIT),
    )(x, lumped_mass)
    out, tri = pl.pallas_call(
        store_kernel,
        name="store",
        out_shape=(jax.ShapeDtypeStruct(modes.shape, F32), jax.ShapeDtypeStruct((K, K), F32)),
        in_specs=[anywhere, anywhere],
        out_specs=(anywhere, anywhere),
        scratch_shapes=[dma((2,))],
        compiler_params=pltpu.CompilerParams(vmem_limit_bytes=STORE_LIMIT),
    )(modes, upper)
    return out.reshape(K, 1, COORDS), tri


STORE_LIMIT = 40 * 2**20
VMEM_LIMIT = 47 * 2**20


def solution(mesh):
    return jax.shard_map(
        body,
        mesh=mesh,
        in_specs=(P("row", "grp"), P("grp", "row")),
        out_specs=(P(None, "grp", "row"), P()),
        check_vma=False,
    )
```

```python
import jax
import jax.numpy as jnp
from jax import lax
from jax.experimental import pallas as pl
from jax.experimental.pallas import tpu as pltpu
from jax.sharding import PartitionSpec as P

MESH = pl.DeviceIdType.MESH
F32 = jnp.float32
BF16 = jnp.bfloat16
K = 256
COORDS = 4096
TILES = 32
FILL = 9
HELD = 12
LAG = 5
B = 64
STEP = 8
SCALE = 1.0 / 1048576
NT = (((1,), (1,)), ((), ()))
NN = (((1,), (0,)), ((), ()))


def split3(v):
    h = v.astype(BF16)
    r = v - h.astype(F32)
    m = r.astype(BF16)
    l = (r - m.astype(F32)).astype(BF16)
    return h, m, l


def mm(a, b, dims):
    return lax.dot_general(a, b, dims, preferred_element_type=F32)


def dot(a, b, dims):
    return lax.dot_general(a, b, dims, precision=lax.Precision.HIGHEST, preferred_element_type=F32)


def eliminate(block):
    rows = lax.broadcasted_iota(jnp.int32, (B, B), 0)
    lanes = lax.broadcasted_iota(jnp.int32, (B, B), 1)
    m = jnp.concatenate([block, jnp.where(rows == lanes, 1.0, 0.0)], axis=1)
    tiles = [m[8 * t:8 * t + 8] for t in range(B // 8)]
    done = []
    full = (8, 2 * B)
    for j in range(0, B, STEP):
        t0, s0 = j // 8, j % 8
        top = tiles[t0]
        row = [jnp.broadcast_to(top[s0 + a:s0 + a + 1, :], full) for a in range(STEP)]
        d = {(a, b): jnp.broadcast_to(top[s0 + a:s0 + a + 1, j + b:j + b + 1], full) for a in range(STEP) for b in range(a + 1)}
        live = [t for t in range(t0, B // 8) if 8 * t + 7 >= j + STEP]
        col = {(t, a): jnp.broadcast_to(tiles[t][:, j + a:j + a + 1], full) for t in live for a in range(STEP)}
        inv = []
        for a in range(STEP):
            inv.append(1.0 / d[a, a])
            root = lax.rsqrt(d[a, a])
            root = root * (1.5 - 0.5 * d[a, a] * root * root)
            done.append((row[a] * root)[0:1])
            for b in range(a + 1, STEP):
                f = d[b, a] * inv[a]
                for k in range(b, STEP):
                    d[k, b] = d[k, b] - d[k, a] * f
                row[b] = row[b] - row[a] * f
                for t in live:
                    col[t, b] = col[t, b] - col[t, a] * f
        scaled = [row[a] * inv[a] for a in range(STEP)]
        for t in live:
            for a in range(STEP):
                tiles[t] = tiles[t] - col[t, a] * scaled[a]
    return jnp.concatenate(done, axis=0)


def keep_upper(t):
    rows = lax.broadcasted_iota(jnp.int32, t.shape, 0)
    lanes = lax.broadcasted_iota(jnp.int32, t.shape, 1)
    return jnp.where(lanes >= rows, t, 0.0)


def pod_kernel(x_ref, w_ref, out_ref, tri_ref, buf, stage, xs, gram, p_ref, tmp, pack, parts, zparts, res,
               y_send, y_recv, z_send, z_recv, red_send, red_recv):
    r = lax.axis_index("row")
    g = lax.axis_index("grp")
    y, zc = r // 16, lax.rem(r, 16)
    phase_of = jnp.where(y < 2, 0, y - 1)

    def dev(x_, y_, zc_):
        return (y_ * 16 + zc_, x_)

    plane = [(dx, dy) for dx in range(4) for dy in range(4) if (dx, dy) != (0, 0)]
    plane.sort(key=lambda p: -(min(p[0], 4 - p[0]) + min(p[1], 4 - p[1])))

    barrier = pltpu.get_barrier_semaphore()

    @pl.loop(1, 16)
    def _(o):
        pl.semaphore_signal(barrier, 1, device_id=dev(g, y, lax.rem(zc + o, 16)), device_id_type=MESH)

    for dx, dy in plane:
        pl.semaphore_signal(barrier, 1, device_id=dev(lax.rem(g + dx, 4), lax.rem(y + dy, 4), zc), device_id_type=MESH)
    pl.semaphore_wait(barrier, 30)

    def block(plane_y, b):
        return x_ref.at[pl.ds(pl.multiple_of((plane_y * 16 + b) * 128, 128), 128)]

    def target(i):
        return lax.rem(zc + lax.rem(i * 7, 15) + 1, 16)

    def along_y(i):
        for d in (1, 3, 2):
            to = lax.rem(y + d, 4)
            pltpu.make_async_remote_copy(
                src_ref=block(to, target(i)), dst_ref=stage.at[d - 1, i], send_sem=y_send, recv_sem=y_recv.at[d - 1, i],
                device_id=dev(g, to, zc), device_id_type=MESH).start()

    def along_z(src, slot, i, which):
        pltpu.make_async_remote_copy(
            src_ref=src, dst_ref=buf.at[slot], send_sem=z_send, recv_sem=z_recv.at[which],
            device_id=dev(g, y, target(i)), device_id_type=MESH).start()

    def forward(d, i, which):
        pltpu.make_async_copy(stage.at[0, 0], stage.at[d - 1, i], y_recv.at[d - 1, i]).wait()
        along_z(stage.at[d - 1, i], lax.rem(y - d + 4, 4) * 16 + zc, i, which)

    def own(i, which):
        along_z(block(y, target(i)), r, i, which)

    def own_column():
        for d in (1, 3, 2):
            to = lax.rem(y + d, 4)
            pltpu.make_async_remote_copy(
                src_ref=block(to, zc), dst_ref=buf.at[r], send_sem=y_send, recv_sem=z_recv.at[phase_of],
                device_id=dev(g, to, zc), device_id_type=MESH).start()
        pltpu.make_async_copy(block(y, zc), buf.at[r], z_recv.at[phase_of]).start()

    @pl.when(y < 2)
    def _():
        other = jnp.where(y == 0, 3, 1)

        @pl.loop(0, LAG)
        def _(i):
            along_y(i)
            own(i, 0)

        @pl.loop(LAG, 15)
        def _(i):
            along_y(i)
            own(i, 0)
            forward(other, i - LAG, 0)

        own_column()

        @pl.loop(15 - LAG, 15)
        def _(i):
            forward(other, i, 0)

    @pl.when(y >= 2)
    def _():
        @pl.loop(0, FILL)
        def _(i):
            along_y(i)
            own(i, phase_of)

        @pl.loop(0, 15)
        def _(i):
            forward(y, i, 0)
            forward(y - 1, i, 0)

            @pl.when(i + FILL < 15)
            def _():
                along_y(i + FILL)

        own_column()

    def send_plane(src, lo, hi):
        d = lax.rem(y - src + 4, 4)

        @pl.when(d != 0)
        def _():
            @pl.loop(lo, hi)
            def _(i):
                forward(d, i, src - 1)

        if hi > FILL:
            @pl.when(d == 0)
            def _():
                @pl.loop(lo, hi)
                def _(i):
                    own(i, src - 1)

    def wait(ref, sem):
        pltpu.make_async_copy(ref, ref, sem).wait()

    def weighted(lo, n, pair):
        v = buf[lo // 4:(lo + n) // 4, pl.ds(pl.multiple_of(pair * 8, 8), 8), :].reshape(n // 8, 2, 8, 128)
        even, odd = v[:, 0], v[:, 1]
        low = lax.broadcasted_iota(jnp.int32, even.shape, 1) < 4
        left = jnp.where(low, even, pltpu.roll(odd, 4, 1)).reshape(n, 128)
        right = jnp.where(low, pltpu.roll(even, 4, 1), odd).reshape(n, 128)
        cols = pl.ds(pl.multiple_of(pair * 256, 256), 256)
        for k, v in enumerate(split3(jnp.concatenate([left, right], axis=1) * jnp.sqrt(w_ref[:, cols]))):
            xs[k, lo:lo + n, cols] = v

    def rows_gram(lo, n):
        end = lo + n
        gram[:3 * n, :end] = jnp.zeros((3 * n, end), F32)

        @pl.loop(0, 4)
        def _(quad):
            for p in range(4):
                weighted(lo, n, quad * 4 + p)
            cols = pl.ds(pl.multiple_of(quad * 1024, 1024), 1024)
            h, m, l = xs[0, lo:end, cols], xs[1, lo:end, cols], xs[2, lo:end, cols]
            gram[:3 * n, :end] += mm(jnp.concatenate([h, m, l], axis=0), xs[0, :end, cols], NT)
            gram[:2 * n, :end] += mm(jnp.concatenate([h, m], axis=0), xs[1, :end, cols], NT)
            gram[:n, :end] += mm(h, xs[2, :end, cols], NT)

        return (gram[2 * n:3 * n, :end] + gram[n:2 * n, :end]) + gram[:n, :end]

    def send(src, dst, i, to):
        pltpu.make_async_remote_copy(src_ref=src, dst_ref=dst, send_sem=red_send.at[i], recv_sem=red_recv.at[i],
                                     device_id=to, device_id_type=MESH).start()

    def part(ref, k, px, py):
        return ref.at[k, pl.ds(pl.multiple_of((px * 4 + py) * 8, 8), 8)]

    def sum_start(k):
        for dx, dy in plane:
            px, py = lax.rem(g + dx, 4), lax.rem(y + dy, 4)
            send(part(pack, k, px, py), parts.at[k, dx * 4 + dy - 1], 3 * k, dev(px, py, zc))

    def sum_second(k):
        wait(parts.at[k], red_recv.at[3 * k])
        mine = part(pack, k, g, y)[...]
        for i in range(15):
            mine = mine + parts[k, i]
        zparts[k, zc] = mine

        @pl.loop(0, 15)
        def _(i):
            send(zparts.at[k, zc], zparts.at[k, zc], 3 * k + 1, dev(g, y, target(i)))

    def sum_third(k):
        wait(zparts.at[k, pl.ds(0, 15)], red_recv.at[3 * k + 1])
        total = zparts[k, 0]
        for i in range(1, 16):
            total = total + zparts[k, i]
        here = part(res, k, g, y)
        here[...] = total * SCALE
        for dx, dy in plane:
            send(here, here, 3 * k + 2, dev(lax.rem(g + dx, 4), lax.rem(y + dy, 4), zc))

    def sum_done(k):
        wait(parts.at[k], red_recv.at[3 * k + 2])

    def reduce_end(k):
        wait(parts.at[k], red_send.at[3 * k])
        wait(parts.at[k], red_send.at[3 * k + 1])
        wait(parts.at[k], red_send.at[3 * k + 2])

    def factor_rows(lo, strip, corner):
        hi = lo + B
        above = p_ref[:lo, :lo]
        side = dot(strip, above, NT)
        both = eliminate(corner - dot(side, side, NT))
        inv = both[:, B:]
        tri_ref[lo:hi, lo:hi] = keep_upper(both[:, :B])
        tri_ref[:lo, lo:hi] = dot(above, strip, NT)
        p_ref[lo:hi, :lo] = -dot(inv, dot(side, above, NN), NN)
        p_ref[lo:hi, lo:hi] = inv

    def project(w3, lo, n, q):
        end = lo + n
        wh, wm, wl = w3
        w_hml = jnp.concatenate([wh, wm, wl], axis=0)
        w_hm = jnp.concatenate([wh, wm], axis=0)
        for i in range(4):
            cols = pl.ds(q * 1024 + i * 256, 256)
            s = mm(w_hml, xs[0, :end, cols], NN)
            t = mm(w_hm, xs[1, :end, cols], NN)
            u = mm(wh, xs[2, :end, cols], NN)
            tmp[:n, i * 256:i * 256 + 256] = (s[2 * n:] + t[n:] + u) + (s[n:2 * n] + t[:n]) + s[:n]
        v = [tmp[:n, k * 128:k * 128 + 128].reshape(n // 8, 8, 128) for k in range(8)]
        sub = lax.broadcasted_iota(jnp.int32, (n // 8, 8, 128), 1)
        for step in (4, 2, 1):
            keep = (sub & step) == 0
            for k in range(8):
                if k & step == 0:
                    a, b = v[k], v[k + step]
                    v[k] = jnp.where(keep, a, pltpu.roll(b, step, 1))
                    v[k + step] = jnp.where(keep, pltpu.roll(a, 8 - step, 1), b)
        for s in range(8):
            out_ref[lo // 8:end // 8, s, 8 * q:8 * q + 8, :] = v[s]

    p_ref[...] = jnp.zeros_like(p_ref)
    tri_ref[...] = jnp.zeros_like(tri_ref)
    send_plane(2, 0, FILL)
    send_plane(2, FILL, 15)

    wait(buf.at[pl.ds(0, 32)], z_recv.at[0])
    pack[0] = rows_gram(0, 128)
    sum_start(0)
    send_plane(3, 0, FILL)
    send_plane(3, FILL, HELD)

    wait(buf.at[pl.ds(32, 16)], z_recv.at[1])
    strip = rows_gram(128, B)
    pack[1, :B] = strip[:, :128]
    pack[1, B:, :B] = strip[:, 128:]
    pack[1, B:, B:] = jnp.zeros((B, B), F32)
    sum_second(0)
    sum_start(1)
    send_plane(3, HELD, 15)
    sum_third(0)
    sum_second(1)

    wait(buf.at[pl.ds(48, 16)], z_recv.at[2])
    strip = rows_gram(192, B)
    pack[2, :B] = strip[:, :128]
    pack[2, B:] = strip[:, 128:]
    sum_start(2)
    sum_third(1)
    sum_done(0)
    both = eliminate(res[0, :B, :B])
    p_ref[:B, :B] = both[:, B:]
    tri_ref[:B, :B] = keep_upper(both[:, :B])
    factor_rows(B, res[0, B:, :B], res[0, B:, B:])
    sum_second(2)
    sum_done(1)
    factor_rows(128, res[1, :B], res[1, B:, :B])
    sum_third(2)
    w3 = split3(p_ref[:192, :192])
    for q in range(4):
        project(w3, 0, 192, q)
    sum_done(2)
    factor_rows(192, jnp.concatenate([res[2, :B], res[2, B:, :B]], axis=1), res[2, B:, B:])
    w3 = split3(p_ref[192:, :])
    for q in range(4):
        project(w3, 192, B, q)

    for k in range(3):
        reduce_end(k)
    wait(buf.at[pl.ds(0, 48)], y_send)
    wait(buf.at[pl.ds(0, 60)], z_send)


def store_kernel(modes_ref, upper_ref, out_ref, tri_ref, sems):
    one = pltpu.make_async_copy(modes_ref, out_ref, sems.at[0])
    two = pltpu.make_async_copy(upper_ref, tri_ref, sems.at[1])
    one.start()
    two.start()
    one.wait()
    two.wait()


def body(snapshots, lumped_mass):
    x = snapshots.reshape(4, 2048, 128).transpose(1, 0, 2).reshape(8192, 128)
    anywhere = pl.BlockSpec(memory_space=pl.ANY)
    vmem = pl.BlockSpec(memory_space=pltpu.VMEM)
    dma = pltpu.SemaphoreType.DMA

    def room(*shape):
        return pltpu.VMEM(shape, F32)

    modes, upper = pl.pallas_call(
        pod_kernel,
        name="pod",
        out_shape=(jax.ShapeDtypeStruct((32, 8, TILES, 128), F32), jax.ShapeDtypeStruct((K, K), F32)),
        in_specs=[anywhere, vmem],
        out_specs=(vmem, vmem),
        scratch_shapes=[
            room(64, 128, 128), room(3, 15, 128, 128), pltpu.VMEM((3, K, COORDS), BF16),
            room(384, K), room(K, K), room(192, 1024),
            room(3, 128, 128), room(3, 15, 8, 128), room(3, 16, 8, 128), room(3, 128, 128),
            dma, dma((3, 15)), dma, dma((3,)), dma((9,)), dma((9,)),
        ],
        compiler_params=pltpu.CompilerParams(collective_id=0, has_side_effects=True, vmem_limit_bytes=VMEM_LIMIT),
    )(x, lumped_mass)
    out, tri = pl.pallas_call(
        store_kernel,
        name="store",
        out_shape=(jax.ShapeDtypeStruct(modes.shape, F32), jax.ShapeDtypeStruct((K, K), F32)),
        in_specs=[anywhere, anywhere],
        out_specs=(anywhere, anywhere),
        scratch_shapes=[dma((2,))],
        compiler_params=pltpu.CompilerParams(vmem_limit_bytes=STORE_LIMIT),
    )(modes, upper)
    return out.reshape(K, 1, COORDS), tri


STORE_LIMIT = 40 * 2**20
VMEM_LIMIT = 47 * 2**20


def solution(mesh):
    return jax.shard_map(
        body,
        mesh=mesh,
        in_specs=(P("row", "grp"), P("grp", "row")),
        out_specs=(P(None, "grp", "row"), P()),
        check_vma=False,
    )
```

```python
import jax
import jax.numpy as jnp
from jax import lax
from jax.experimental import pallas as pl
from jax.experimental.pallas import tpu as pltpu
from jax.sharding import PartitionSpec as P

MESH = pl.DeviceIdType.MESH
F32 = jnp.float32
BF16 = jnp.bfloat16
K = 256
COORDS = 4096
TILES = 32
FILL = 12
HELD = 14
LAG = 5
B = 64
STEP = 8
SCALE = 1.0 / 1048576
NT = (((1,), (1,)), ((), ()))
NN = (((1,), (0,)), ((), ()))


def split3(v):
    h = v.astype(BF16)
    r = v - h.astype(F32)
    m = r.astype(BF16)
    l = (r - m.astype(F32)).astype(BF16)
    return h, m, l


def mm(a, b, dims):
    return lax.dot_general(a, b, dims, preferred_element_type=F32)


def dot(a, b, dims):
    return lax.dot_general(a, b, dims, precision=lax.Precision.HIGHEST, preferred_element_type=F32)


def eliminate(block):
    rows = lax.broadcasted_iota(jnp.int32, (B, B), 0)
    lanes = lax.broadcasted_iota(jnp.int32, (B, B), 1)
    m = jnp.concatenate([block, jnp.where(rows == lanes, 1.0, 0.0)], axis=1)
    tiles = [m[8 * t:8 * t + 8] for t in range(B // 8)]
    done = []
    full = (8, 2 * B)
    for j in range(0, B, STEP):
        t0, s0 = j // 8, j % 8
        top = tiles[t0]
        row = [jnp.broadcast_to(top[s0 + a:s0 + a + 1, :], full) for a in range(STEP)]
        d = {(a, b): jnp.broadcast_to(top[s0 + a:s0 + a + 1, j + b:j + b + 1], full) for a in range(STEP) for b in range(a + 1)}
        live = [t for t in range(t0, B // 8) if 8 * t + 7 >= j + STEP]
        col = {(t, a): jnp.broadcast_to(tiles[t][:, j + a:j + a + 1], full) for t in live for a in range(STEP)}
        inv = []
        for a in range(STEP):
            inv.append(1.0 / d[a, a])
            root = lax.rsqrt(d[a, a])
            root = root * (1.5 - 0.5 * d[a, a] * root * root)
            done.append((row[a] * root)[0:1])
            for b in range(a + 1, STEP):
                f = d[b, a] * inv[a]
                for k in range(b, STEP):
                    d[k, b] = d[k, b] - d[k, a] * f
                row[b] = row[b] - row[a] * f
                for t in live:
                    col[t, b] = col[t, b] - col[t, a] * f
        scaled = [row[a] * inv[a] for a in range(STEP)]
        for t in live:
            for a in range(STEP):
                tiles[t] = tiles[t] - col[t, a] * scaled[a]
    return jnp.concatenate(done, axis=0)


def keep_upper(t):
    rows = lax.broadcasted_iota(jnp.int32, t.shape, 0)
    lanes = lax.broadcasted_iota(jnp.int32, t.shape, 1)
    return jnp.where(lanes >= rows, t, 0.0)


def pod_kernel(x_ref, w_ref, out_ref, tri_ref, buf, stage, xs, gram, p_ref, tmp, pack, parts, zparts, res,
               y_send, y_recv, z_send, z_recv, red_send, red_recv):
    r = lax.axis_index("row")
    g = lax.axis_index("grp")
    y, zc = r // 16, lax.rem(r, 16)
    phase_of = jnp.where(y < 2, 0, y - 1)

    def dev(x_, y_, zc_):
        return (y_ * 16 + zc_, x_)

    plane = [(dx, dy) for dx in range(4) for dy in range(4) if (dx, dy) != (0, 0)]
    plane.sort(key=lambda p: -(min(p[0], 4 - p[0]) + min(p[1], 4 - p[1])))

    barrier = pltpu.get_barrier_semaphore()

    @pl.loop(1, 16)
    def _(o):
        pl.semaphore_signal(barrier, 1, device_id=dev(g, y, lax.rem(zc + o, 16)), device_id_type=MESH)

    for dx, dy in plane:
        pl.semaphore_signal(barrier, 1, device_id=dev(lax.rem(g + dx, 4), lax.rem(y + dy, 4), zc), device_id_type=MESH)
    pl.semaphore_wait(barrier, 30)

    def block(plane_y, b):
        return x_ref.at[pl.ds(pl.multiple_of((plane_y * 16 + b) * 128, 128), 128)]

    def target(i):
        return lax.rem(zc + lax.rem(i * 7, 15) + 1, 16)

    def along_y(i):
        for d in (1, 3, 2):
            to = lax.rem(y + d, 4)
            pltpu.make_async_remote_copy(
                src_ref=block(to, target(i)), dst_ref=stage.at[d - 1, i], send_sem=y_send, recv_sem=y_recv.at[d - 1, i],
                device_id=dev(g, to, zc), device_id_type=MESH).start()

    def along_z(src, slot, i, which):
        pltpu.make_async_remote_copy(
            src_ref=src, dst_ref=buf.at[slot], send_sem=z_send, recv_sem=z_recv.at[which],
            device_id=dev(g, y, target(i)), device_id_type=MESH).start()

    def forward(d, i, which):
        pltpu.make_async_copy(stage.at[0, 0], stage.at[d - 1, i], y_recv.at[d - 1, i]).wait()
        along_z(stage.at[d - 1, i], lax.rem(y - d + 4, 4) * 16 + zc, i, which)

    def own(i, which):
        along_z(block(y, target(i)), r, i, which)

    def own_column():
        for d in (1, 3, 2):
            to = lax.rem(y + d, 4)
            pltpu.make_async_remote_copy(
                src_ref=block(to, zc), dst_ref=buf.at[r], send_sem=y_send, recv_sem=z_recv.at[phase_of],
                device_id=dev(g, to, zc), device_id_type=MESH).start()
        pltpu.make_async_copy(block(y, zc), buf.at[r], z_recv.at[phase_of]).start()

    @pl.when(y < 2)
    def _():
        other = jnp.where(y == 0, 3, 1)

        @pl.loop(0, LAG)
        def _(i):
            along_y(i)
            own(i, 0)

        @pl.loop(LAG, 15)
        def _(i):
            along_y(i)
            own(i, 0)
            forward(other, i - LAG, 0)

        own_column()

        @pl.loop(15 - LAG, 15)
        def _(i):
            forward(other, i, 0)

    @pl.when(y >= 2)
    def _():
        @pl.loop(0, FILL)
        def _(i):
            along_y(i)
            own(i, phase_of)

        @pl.loop(0, 15)
        def _(i):
            forward(y, i, 0)
            forward(y - 1, i, 0)

            @pl.when(i + FILL < 15)
            def _():
                along_y(i + FILL)

        own_column()

    def send_plane(src, lo, hi):
        d = lax.rem(y - src + 4, 4)

        @pl.when(d != 0)
        def _():
            @pl.loop(lo, hi)
            def _(i):
                forward(d, i, src - 1)

        if hi > FILL:
            @pl.when(d == 0)
            def _():
                @pl.loop(lo, hi)
                def _(i):
                    own(i, src - 1)

    def wait(ref, sem):
        pltpu.make_async_copy(ref, ref, sem).wait()

    def weighted(lo, n, pair):
        v = buf[lo // 4:(lo + n) // 4, pl.ds(pl.multiple_of(pair * 8, 8), 8), :].reshape(n // 8, 2, 8, 128)
        even, odd = v[:, 0], v[:, 1]
        low = lax.broadcasted_iota(jnp.int32, even.shape, 1) < 4
        left = jnp.where(low, even, pltpu.roll(odd, 4, 1)).reshape(n, 128)
        right = jnp.where(low, pltpu.roll(even, 4, 1), odd).reshape(n, 128)
        cols = pl.ds(pl.multiple_of(pair * 256, 256), 256)
        for k, v in enumerate(split3(jnp.concatenate([left, right], axis=1) * jnp.sqrt(w_ref[:, cols]))):
            xs[k, lo:lo + n, cols] = v

    def rows_gram(lo, n):
        end = lo + n
        gram[:3 * n, :end] = jnp.zeros((3 * n, end), F32)

        @pl.loop(0, 4)
        def _(quad):
            for p in range(4):
                weighted(lo, n, quad * 4 + p)
            cols = pl.ds(pl.multiple_of(quad * 1024, 1024), 1024)
            h, m, l = xs[0, lo:end, cols], xs[1, lo:end, cols], xs[2, lo:end, cols]
            gram[:3 * n, :end] += mm(jnp.concatenate([h, m, l], axis=0), xs[0, :end, cols], NT)
            gram[:2 * n, :end] += mm(jnp.concatenate([h, m], axis=0), xs[1, :end, cols], NT)
            gram[:n, :end] += mm(h, xs[2, :end, cols], NT)

        return (gram[2 * n:3 * n, :end] + gram[n:2 * n, :end]) + gram[:n, :end]

    def send(src, dst, i, to):
        pltpu.make_async_remote_copy(src_ref=src, dst_ref=dst, send_sem=red_send.at[i], recv_sem=red_recv.at[i],
                                     device_id=to, device_id_type=MESH).start()

    def part(ref, k, px, py):
        return ref.at[k, pl.ds(pl.multiple_of((px * 4 + py) * 8, 8), 8)]

    def sum_start(k):
        for dx, dy in plane:
            px, py = lax.rem(g + dx, 4), lax.rem(y + dy, 4)
            send(part(pack, k, px, py), parts.at[k, dx * 4 + dy - 1], 3 * k, dev(px, py, zc))

    def sum_second(k):
        wait(parts.at[k], red_recv.at[3 * k])
        mine = part(pack, k, g, y)[...]
        for i in range(15):
            mine = mine + parts[k, i]
        zparts[k, zc] = mine

        @pl.loop(0, 15)
        def _(i):
            send(zparts.at[k, zc], zparts.at[k, zc], 3 * k + 1, dev(g, y, target(i)))

    def sum_third(k):
        wait(zparts.at[k, pl.ds(0, 15)], red_recv.at[3 * k + 1])
        total = zparts[k, 0]
        for i in range(1, 16):
            total = total + zparts[k, i]
        here = part(res, k, g, y)
        here[...] = total * SCALE
        for dx, dy in plane:
            send(here, here, 3 * k + 2, dev(lax.rem(g + dx, 4), lax.rem(y + dy, 4), zc))

    def sum_done(k):
        wait(parts.at[k], red_recv.at[3 * k + 2])

    def reduce_end(k):
        wait(parts.at[k], red_send.at[3 * k])
        wait(parts.at[k], red_send.at[3 * k + 1])
        wait(parts.at[k], red_send.at[3 * k + 2])

    def factor_rows(lo, strip, corner):
        hi = lo + B
        above = p_ref[:lo, :lo]
        side = dot(strip, above, NT)
        both = eliminate(corner - dot(side, side, NT))
        inv = both[:, B:]
        tri_ref[lo:hi, lo:hi] = keep_upper(both[:, :B])
        tri_ref[:lo, lo:hi] = dot(above, strip, NT)
        p_ref[lo:hi, :lo] = -dot(inv, dot(side, above, NN), NN)
        p_ref[lo:hi, lo:hi] = inv

    def project(w3, lo, n, q):
        end = lo + n
        wh, wm, wl = w3
        w_hml = jnp.concatenate([wh, wm, wl], axis=0)
        w_hm = jnp.concatenate([wh, wm], axis=0)
        for i in range(4):
            cols = pl.ds(q * 1024 + i * 256, 256)
            s = mm(w_hml, xs[0, :end, cols], NN)
            t = mm(w_hm, xs[1, :end, cols], NN)
            u = mm(wh, xs[2, :end, cols], NN)
            tmp[:n, i * 256:i * 256 + 256] = (s[2 * n:] + t[n:] + u) + (s[n:2 * n] + t[:n]) + s[:n]
        v = [tmp[:n, k * 128:k * 128 + 128].reshape(n // 8, 8, 128) for k in range(8)]
        sub = lax.broadcasted_iota(jnp.int32, (n // 8, 8, 128), 1)
        for step in (4, 2, 1):
            keep = (sub & step) == 0
            for k in range(8):
                if k & step == 0:
                    a, b = v[k], v[k + step]
                    v[k] = jnp.where(keep, a, pltpu.roll(b, step, 1))
                    v[k + step] = jnp.where(keep, pltpu.roll(a, 8 - step, 1), b)
        for s in range(8):
            out_ref[lo // 8:end // 8, s, 8 * q:8 * q + 8, :] = v[s]

    p_ref[...] = jnp.zeros_like(p_ref)
    tri_ref[...] = jnp.zeros_like(tri_ref)
    send_plane(2, 0, FILL)
    send_plane(2, FILL, 15)

    wait(buf.at[pl.ds(0, 32)], z_recv.at[0])
    pack[0] = rows_gram(0, 128)
    sum_start(0)
    send_plane(3, 0, FILL)
    send_plane(3, FILL, HELD)

    wait(buf.at[pl.ds(32, 16)], z_recv.at[1])
    strip = rows_gram(128, B)
    pack[1, :B] = strip[:, :128]
    pack[1, B:, :B] = strip[:, 128:]
    pack[1, B:, B:] = jnp.zeros((B, B), F32)
    sum_second(0)
    sum_start(1)
    send_plane(3, HELD, 15)
    sum_third(0)
    sum_second(1)

    wait(buf.at[pl.ds(48, 16)], z_recv.at[2])
    strip = rows_gram(192, B)
    pack[2, :B] = strip[:, :128]
    pack[2, B:] = strip[:, 128:]
    sum_start(2)
    sum_third(1)
    sum_done(0)
    both = eliminate(res[0, :B, :B])
    p_ref[:B, :B] = both[:, B:]
    tri_ref[:B, :B] = keep_upper(both[:, :B])
    factor_rows(B, res[0, B:, :B], res[0, B:, B:])
    sum_second(2)
    sum_done(1)
    factor_rows(128, res[1, :B], res[1, B:, :B])
    sum_third(2)
    w3 = split3(p_ref[:192, :192])
    for q in range(4):
        project(w3, 0, 192, q)
    sum_done(2)
    factor_rows(192, jnp.concatenate([res[2, :B], res[2, B:, :B]], axis=1), res[2, B:, B:])
    w3 = split3(p_ref[192:, :])
    for q in range(4):
        project(w3, 192, B, q)

    for k in range(3):
        reduce_end(k)
    wait(buf.at[pl.ds(0, 48)], y_send)
    wait(buf.at[pl.ds(0, 60)], z_send)


def store_kernel(modes_ref, upper_ref, out_ref, tri_ref, sems):
    one = pltpu.make_async_copy(modes_ref, out_ref, sems.at[0])
    two = pltpu.make_async_copy(upper_ref, tri_ref, sems.at[1])
    one.start()
    two.start()
    one.wait()
    two.wait()


def body(snapshots, lumped_mass):
    x = snapshots.reshape(4, 2048, 128).transpose(1, 0, 2).reshape(8192, 128)
    anywhere = pl.BlockSpec(memory_space=pl.ANY)
    vmem = pl.BlockSpec(memory_space=pltpu.VMEM)
    dma = pltpu.SemaphoreType.DMA

    def room(*shape):
        return pltpu.VMEM(shape, F32)

    modes, upper = pl.pallas_call(
        pod_kernel,
        name="pod",
        out_shape=(jax.ShapeDtypeStruct((32, 8, TILES, 128), F32), jax.ShapeDtypeStruct((K, K), F32)),
        in_specs=[anywhere, vmem],
        out_specs=(vmem, vmem),
        scratch_shapes=[
            room(64, 128, 128), room(3, 15, 128, 128), pltpu.VMEM((3, K, COORDS), BF16),
            room(384, K), room(K, K), room(192, 1024),
            room(3, 128, 128), room(3, 15, 8, 128), room(3, 16, 8, 128), room(3, 128, 128),
            dma, dma((3, 15)), dma, dma((3,)), dma((9,)), dma((9,)),
        ],
        compiler_params=pltpu.CompilerParams(collective_id=0, has_side_effects=True, vmem_limit_bytes=VMEM_LIMIT),
    )(x, lumped_mass)
    out, tri = pl.pallas_call(
        store_kernel,
        name="store",
        out_shape=(jax.ShapeDtypeStruct(modes.shape, F32), jax.ShapeDtypeStruct((K, K), F32)),
        in_specs=[anywhere, anywhere],
        out_specs=(anywhere, anywhere),
        scratch_shapes=[dma((2,))],
        compiler_params=pltpu.CompilerParams(vmem_limit_bytes=STORE_LIMIT),
    )(modes, upper)
    return out.reshape(K, 1, COORDS), tri


STORE_LIMIT = 40 * 2**20
VMEM_LIMIT = 47 * 2**20


def solution(mesh):
    return jax.shard_map(
        body,
        mesh=mesh,
        in_specs=(P("row", "grp"), P("grp", "row")),
        out_specs=(P(None, "grp", "row"), P()),
        check_vma=False,
    )
```
